128 devices in a mesh: scan: 16 (over z, x), tile: 8 (over y, core).
Axes of the slice: x: 4, y: 4, z: 4, core: 2. Of those that a mesh axis runs over, the one named last changes fastest.
Arguments:
- object_planes: float32 [2, 8192, 8192], P(None, 'scan', 'tile'), may hold values from -5 to 5
- probe_planes: float32 [2, 512, 512], replicated, may hold values from -5 to 5
- amplitudes: float32 [768, 512, 512], P(('scan', 'tile')), may hold values from 0.3 to 2
- off_rows: int32 [768], P(('scan', 'tile')), may hold values from 0 to 511
- off_cols: int32 [768], P(('scan', 'tile')), may hold values from 0 to 1023
Outputs:
- object_grad: float32 [2, 8192, 8192], P(None, 'scan', 'tile')
- probe_grad: float32 [2, 512, 512], replicated
The draws below stay inside these ranges and needn't reach their ends.
Inputs may be any that keep to these rules, and one draw needn't show every extreme that they name: off_rows[k] is the row offset of position k inside the tile of its device, the device k // 6 in the order scan then tile. off_cols[k] is the column offset of position k inside the tile of its device.
All inputs are finite; a program needn't handle non-finite values.
Results may differ from the reference program's by a relative error of at most 0.0054.
The reference program's roundings to bfloat16 on the way count: a program that leaves them out, or rounds other values in their place, can miss the bound.
Values sent between devices are 32-bit elements; how exact they have to be, the bound alone decides.
No kernel may reach another device: no remote copies, remote signals or barrier semaphores. Data moves between devices by JAX's collectives and lax.ppermute only.
A program may use at most 128 MiB of HBM per device.

```python
import jax
import jax.numpy as jnp
from jax import lax

M = 512
PPD = 6
TR = 512
TC = 1024
NY = 8192
NX = 8192
NPOS = 768
N_TILE = 8


def set_ends(entries, stream_key, least, largest):
    longest = entries.shape.index(max(entries.shape))
    spots = []
    for shift in (0, 1):
        where = [jax.random.randint(jax.random.fold_in(stream_key, axis), (), 0, length) for axis, length in enumerate(entries.shape)]
        where[longest] = (where[longest] + shift) % entries.shape[longest]
        spots.append(tuple(where))
    return entries.at[spots[0]].set(least).at[spots[1]].set(largest)


def block_levels(rng, dims, split, smallest, top_value):
    def one(dim, parts):
        draws = jax.random.uniform(jax.random.fold_in(jax.random.fold_in(rng, 6), dim), (parts,), jnp.float32, smallest / len(split), top_value / len(split))
        return jnp.repeat(jnp.exp(draws), dims[dim] // parts).reshape((-1,) + (1,) * (len(dims) - dim - 1))

    factor_of = one(*split[0])
    for cut in split[1:]:
        factor_of = factor_of * one(*cut)
    return factor_of


def scatter_about(key, extent, scale, bound, pieces=(), kind=jnp.bfloat16):
    loudness = block_levels(key, extent, pieces, -0.22, 0.18) if pieces else 1.0
    array = jax.random.normal(key, extent, jnp.float32) * scale * loudness
    return jnp.minimum(jnp.maximum(array, -bound), bound).astype(kind)


def setup_inputs(seed: int = 0) -> dict:
    seeds = jax.random.split(jax.random.key(seed), 6)
    return {
        "object_planes": scatter_about(seeds[0], (2, NY, NX), 0.7, 5.0, ((1, 16), (2, 8)), jnp.float32),
        "probe_planes": scatter_about(seeds[1], (2, M, M), 0.7, 5.0, (), jnp.float32),
        "amplitudes": jnp.clip(0.3 + 1.7 * jax.random.uniform(seeds[2], (NPOS, M, M), jnp.float32) ** block_levels(seeds[2], (NPOS, M, M), ((0, 128),), -0.2, 0.2), 0.3, 2.0),
        "off_rows": set_ends(jax.random.randint(seeds[3], (NPOS,), 0, TR), jax.random.fold_in(seeds[3], 1), 0, TR - 1).astype(jnp.int32),
        "off_cols": set_ends(jax.random.randint(seeds[4], (NPOS,), 0, TC), jax.random.fold_in(seeds[4], 1), 0, TC - 1).astype(jnp.int32),
    }


def dft_tables(width):
    counter = jnp.arange(width, dtype=jnp.int32)
    product = counter[:, None] * counter[None, :] % width
    angles = product.astype(jnp.float32) * (2.0 * 3.141592653589793 / width)
    norm_scale = 1.0 / jnp.sqrt(jnp.float32(width))
    return ((jnp.cos(angles) * norm_scale).astype(jnp.bfloat16), (jnp.sin(angles) * norm_scale).astype(jnp.bfloat16))

def matmul(first, second):
    return jnp.dot(first, second, preferred_element_type=jnp.float32)

def apply_left(cosine, sine, real_part, imag_part, sign):
    return (matmul(cosine, real_part) - sign * matmul(sine, imag_part), matmul(cosine, imag_part) + sign * matmul(sine, real_part))

def apply_right(cosine, sine, real_part, imag_part, sign):
    return (matmul(real_part, cosine) - sign * matmul(imag_part, sine), matmul(imag_part, cosine) + sign * matmul(real_part, sine))

def position_wave(patch_real, patch_imag, probe_real, probe_imag, amplitude, cosine, sine):
    psi_real = (probe_real * patch_real - probe_imag * patch_imag).astype(jnp.bfloat16)
    psi_imag = (probe_real * patch_imag + probe_imag * patch_real).astype(jnp.bfloat16)
    half_real, half_imag = apply_left(cosine, sine, psi_real, psi_imag, -1.0)
    far_real, far_imag = apply_right(cosine, sine, half_real.astype(jnp.bfloat16), half_imag.astype(jnp.bfloat16), -1.0)
    magnitude = jnp.sqrt(far_real * far_real + far_imag * far_imag)
    factor = 1.0 - amplitude / jnp.maximum(magnitude, 0.5)
    misfit_real = (far_real * factor).astype(jnp.bfloat16)
    misfit_imag = (far_imag * factor).astype(jnp.bfloat16)
    back_real, back_imag = apply_left(cosine, sine, misfit_real, misfit_imag, 1.0)
    return apply_right(cosine, sine, back_real.astype(jnp.bfloat16), back_imag.astype(jnp.bfloat16), 1.0)

def reference(object_planes, probe_planes, amplitudes, off_rows, off_cols):
    cosine, sine = dft_tables(M)
    wrapped = jnp.concatenate([object_planes, object_planes[:, :M, :]], axis=1)
    wrapped = jnp.concatenate([wrapped, wrapped[:, :, :M]], axis=2)
    probe_real = probe_planes[0]
    probe_imag = probe_planes[1]

    def visit(carried, inputs):
        gradient, probe_sum = carried
        amplitude, row_off, col_off, position = inputs
        device = position // PPD
        row_start = device // N_TILE * TR + row_off
        col_start = device % N_TILE * TC + col_off
        anchor = jnp.zeros((), jnp.int32)
        patch = lax.dynamic_slice(wrapped, (anchor, row_start, col_start), (2, M, M))
        wave_real, wave_imag = position_wave(patch[0], patch[1], probe_real, probe_imag, amplitude, cosine, sine)
        update = jnp.stack([probe_real * wave_real + probe_imag * wave_imag, probe_real * wave_imag - probe_imag * wave_real])
        current = lax.dynamic_slice(gradient, (anchor, row_start, col_start), (2, M, M))
        gradient = lax.dynamic_update_slice(gradient, current + update, (anchor, row_start, col_start))
        probe_sum = probe_sum + jnp.stack([patch[0] * wave_real + patch[1] * wave_imag, patch[0] * wave_imag - patch[1] * wave_real])
        return ((gradient, probe_sum), None)
    positions = jnp.arange(NPOS, dtype=jnp.int32)
    start = (jnp.zeros(wrapped.shape, jnp.float32), jnp.zeros((2, M, M), jnp.float32))
    (gradient, probe_sum), unused = lax.scan(visit, start, (amplitudes, off_rows, off_cols, positions))
    gradient = gradient.at[:, :, :M].add(gradient[:, :, NX:])
    gradient = gradient[:, :, :NX]
    gradient = gradient.at[:, :M, :].add(gradient[:, NY:, :])
    gradient = gradient[:, :NY, :]
    return (gradient, probe_sum / jnp.sqrt(jnp.float32(NPOS)))
```

```python
import jax
import jax.numpy as jnp
import ml_dtypes
import numpy as np
from jax import lax
from jax.sharding import PartitionSpec as P
from jax.experimental import pallas as pl
from jax.experimental.pallas import tpu as pltpu

M = 512
Q4 = 128


def kernel_tables():
    counter = np.arange(M, dtype=np.int64)
    product = counter[:, None] * counter[None, :] % M
    angles = product.astype(np.float32) * np.float32(2.0 * 3.141592653589793 / M)
    norm_scale = np.float32(1.0) / np.sqrt(np.float32(M))
    cosine, sine = np.cos(angles) * norm_scale, np.sin(angles) * norm_scale
    classes = range(4)
    first = np.concatenate([np.arange(m, Q4, 4) for m in classes])
    c, s = cosine[first], sine[first]
    left1 = np.stack([np.block([[c[:, m::4], s[:, m::4]], [-s[:, m::4], c[:, m::4]]]) for m in classes])
    order = np.concatenate([np.arange(m, M, 4) for m in classes])
    c, s = cosine[:, order], sine[:, order]
    right2 = np.block([[c, -s], [s, c]])
    c, s = cosine[:Q4], sine[:Q4]
    left3 = np.stack([np.block([[c[:, m::4], -s[:, m::4]], [s[:, m::4], c[:, m::4]]]) for m in classes])
    c, s = cosine[:, :Q4], sine[:, :Q4]
    right4 = np.stack([np.block([[c[m::4], s[m::4]], [-s[m::4], c[m::4]]]) for m in classes])
    return [jnp.asarray(t.astype(ml_dtypes.bfloat16)) for t in (left1, right2, left3, right4)]


def mm(a, b):
    return jnp.dot(a, b, preferred_element_type=jnp.float32)


def butterfly(e, sign):
    (r0, i0), (r1, i1), (r2, i2), (r3, i3) = e
    ar, ai, br, bi = r0 + r2, i0 + i2, r0 - r2, i0 - i2
    cr, ci, dr, di = r1 + r3, i1 + i3, r1 - r3, i1 - i3
    plus = (br - di, bi + dr)
    minus = (br + di, bi - dr)
    one, three = (plus, minus) if sign > 0 else (minus, plus)
    return [(ar + cr, ai + ci), one, (ar - cr, ai - ci), three]


def spans(pieces, vmem):
    for ref, row, col in pieces:
        for b in range(ref.shape[2] // 128):
            there = vmem.at[:, col // 128 + b, row:row + ref.shape[1], :]
            yield ref.at[:, :, 128 * b:128 * (b + 1)], there


def kernel(row_ref, col_ref, own, low_left, far_left, low_right, far_right, beside, corner_near, corner_far,
           probe, probe4, amp, left1, right2, left3, right4,
           g_own, g_left, g_right, g_beside, g_corner, psum,
           ext, grad, zs, ps, es, hs, qs, xs, gs, sems):
    step = pl.program_id(0)
    last = pl.num_programs(0) - 1
    rows = own.shape[1]
    cols = own.shape[2]
    wide = ext.shape[1]
    near = rows + low_left.shape[1]
    inputs = (
        (own, 0, 0), (low_left, rows, 0), (far_left, near, 0), (low_right, rows, M), (far_right, near, M),
        (beside, 0, cols), (corner_near, rows, cols), (corner_far, near, cols),
    )
    outputs = ((g_own, 0, 0), (g_left, rows, 0), (g_right, rows, M), (g_beside, 0, cols), (g_corner, rows, cols))

    @pl.when(step == 0)
    def _():
        for n, (src, dst) in enumerate(spans(inputs, ext)):
            pltpu.make_async_copy(src, dst, sems.at[n]).start()

        def clear(i, _):
            base = pl.multiple_of(i * 8, 8)
            for p in range(2):
                for b in range(wide):
                    grad[p, b, pl.ds(base, 8), :] = jnp.zeros((8, 128), jnp.float32)
            return 0
        lax.fori_loop(0, grad.shape[2] // 8, clear, 0)

        def clear2(i, _):
            base = pl.multiple_of(i * 8, 8)
            for p in range(2):
                psum[p, pl.ds(base, 8), :] = jnp.zeros((8, M), jnp.float32)
            return 0
        lax.fori_loop(0, M // 8, clear2, 0)
        for n, (src, dst) in enumerate(spans(inputs, ext)):
            pltpu.make_async_copy(src, dst, sems.at[n]).wait()

    r = row_ref[step]
    c = col_ref[step]
    cb = c // 128
    dc = c - cb * 128
    R = 128

    def take(i, _):
        base = pl.multiple_of(i * R, R)
        lane = lax.broadcasted_iota(jnp.int32, (R, 128), 1)
        keep = lane < 128 - dc
        for p in range(2):
            parts = [
                pltpu.roll(ext[p, cb + b, pl.ds(r + base, R), :], 128 - dc, 1)
                for b in range(5)
            ]
            for b in range(4):
                zs[p, b, pl.ds(base, R), :] = jnp.where(keep, parts[b], parts[b + 1])
        return 0
    lax.fori_loop(0, M // R, take, 0)

    def psi(i, _):
        base = pl.multiple_of(i * 16, 16)
        for m in range(4):
            for b in range(4):
                at = slice(128 * b, 128 * (b + 1))
                zr = zs[0, b, pl.ds(base * 4 + m, 16, stride=4), :]
                zi = zs[1, b, pl.ds(base * 4 + m, 16, stride=4), :]
                pr = probe4[0, m, pl.ds(base, 16), at]
                pi = probe4[1, m, pl.ds(base, 16), at]
                ps[m, pl.ds(base, 16), at] = (pr * zr - pi * zi).astype(jnp.bfloat16)
                ps[m, pl.ds(base + Q4, 16), at] = (pr * zi + pi * zr).astype(jnp.bfloat16)
        return 0
    lax.fori_loop(0, Q4 // 16, psi, 0)

    for m in range(4):
        es[m] = mm(left1[m], ps[m])

    def half(i, _):
        base = pl.multiple_of(i * 16, 16)
        e = [(es[m, pl.ds(base, 16), :], es[m, pl.ds(base + Q4, 16), :]) for m in range(4)]
        for j, (re, im) in enumerate(butterfly(e, -1)):
            hs[pl.ds(base + Q4 * j, 16), 0:M] = re.astype(jnp.bfloat16)
            hs[pl.ds(base + Q4 * j, 16), M:] = im.astype(jnp.bfloat16)
        return 0
    lax.fori_loop(0, Q4 // 16, half, 0)

    qs[...] = mm(hs[...], right2[...])

    def chi(i, _):
        base = pl.multiple_of(i * 32, 32)
        j, m = i // 4, i % 4
        fr = qs[pl.ds(base, 32), 0:M]
        fi = qs[pl.ds(base, 32), M:]
        inverse = lax.rsqrt(fr * fr + fi * fi)
        factor = 1.0 - amp[0, pl.ds(base, 32), :] * jnp.minimum(inverse, 2.0)
        to = pl.multiple_of(j * 32, 32)
        xs[m, pl.ds(to, 32), :] = (fr * factor).astype(jnp.bfloat16)
        xs[m, pl.ds(to + Q4, 32), :] = (fi * factor).astype(jnp.bfloat16)
        return 0
    lax.fori_loop(0, M // 32, chi, 0)

    for m in range(4):
        es[m] = mm(left3[m], xs[m])

    def back(i, _):
        base = pl.multiple_of(i * 16, 16)
        e = [(es[m, pl.ds(base, 16), :], es[m, pl.ds(base + Q4, 16), :]) for m in range(4)]
        for j, (re, im) in enumerate(butterfly(e, 1)):
            re = re.astype(jnp.bfloat16)
            im = im.astype(jnp.bfloat16)
            for m in range(4):
                gs[m, pl.ds(base + Q4 * j, 16), 0:Q4] = re[:, Q4 * m:Q4 * (m + 1)]
                gs[m, pl.ds(base + Q4 * j, 16), Q4:] = im[:, Q4 * m:Q4 * (m + 1)]
        return 0
    lax.fori_loop(0, Q4 // 16, back, 0)

    for m in range(4):
        qs[:, 256 * m:256 * (m + 1)] = mm(gs[m], right4[m])

    def finish(i, _):
        N = 16
        base = pl.multiple_of(i * N, N)
        at = pl.ds(base, N)
        lane = lax.broadcasted_iota(jnp.int32, (N, 128), 1)
        keep = lane >= dc
        e = [(qs[at, 256 * m:256 * m + Q4], qs[at, 256 * m + Q4:256 * (m + 1)]) for m in range(4)]
        old = [[grad[p, cb + b, pl.ds(r + base, N), :] for b in range(5)] for p in range(2)]
        sums = [[psum[p, at, Q4 * j:Q4 * (j + 1)] for j in range(4)] for p in range(2)]
        rolled = ([], [])
        for j, (wr, wi) in enumerate(butterfly(e, 1)):
            pr = probe[0, at, Q4 * j:Q4 * (j + 1)]
            pi = probe[1, at, Q4 * j:Q4 * (j + 1)]
            zr = zs[0, j, at, :]
            zi = zs[1, j, at, :]
            sums[0][j] += zr * wr + zi * wi
            sums[1][j] += zr * wi - zi * wr
            rolled[0].append(pltpu.roll(pr * wr + pi * wi, dc, 1))
            rolled[1].append(pltpu.roll(pr * wi - pi * wr, dc, 1))
        zero = jnp.zeros((N, 128), jnp.float32)
        for p in range(2):
            u = [zero] + rolled[p] + [zero]
            for b in range(5):
                grad[p, cb + b, pl.ds(r + base, N), :] = old[p][b] + jnp.where(keep, u[b + 1], u[b])
            for j in range(4):
                psum[p, at, Q4 * j:Q4 * (j + 1)] = sums[p][j]
        return 0
    lax.fori_loop(0, M // 16, finish, 0, unroll=4)

    @pl.when(step == last)
    def _():
        for n, (dst, src) in enumerate(spans(outputs, grad)):
            pltpu.make_async_copy(src, dst, sems.at[n]).start()
        for n, (dst, src) in enumerate(spans(outputs, grad)):
            pltpu.make_async_copy(src, dst, sems.at[n]).wait()


def positions(off_rows, off_cols, objects, probe, amps, tables):
    count = amps.shape[0]
    rows, cols = objects[0].shape[1:]
    f32, bf16 = jnp.float32, jnp.bfloat16
    anyspec = pl.BlockSpec(memory_space=pl.ANY)
    whole = lambda shape: pl.BlockSpec(shape, lambda i, *_: (0,) * len(shape))
    probe4 = probe.reshape(2, Q4, 4, M).transpose(0, 2, 1, 3)
    return pl.pallas_call(
        kernel,
        grid_spec=pltpu.PrefetchScalarGridSpec(
            num_scalar_prefetch=2,
            grid=(count,),
            in_specs=[
                *[anyspec] * len(objects),
                whole((2, M, M)), whole((2, 4, Q4, M)),
                pl.BlockSpec((1, M, M), lambda i, *_: (i, 0, 0)),
                whole((4, 256, 256)), whole((1024, 1024)), whole((4, 256, 256)), whole((4, 256, 256)),
            ],
            out_specs=[*[anyspec] * 5, whole((2, M, M))],
            scratch_shapes=[
                pltpu.VMEM((2, (cols + M) // 128, rows + M, 128), f32),
                pltpu.VMEM((2, (cols + M) // 128, rows + M, 128), f32),
                pltpu.VMEM((2, 4, M, 128), f32),
                pltpu.VMEM((4, 256, M), bf16),
                pltpu.VMEM((4, 256, M), f32),
                pltpu.VMEM((M, 2 * M), bf16),
                pltpu.VMEM((M, 2 * M), f32),
                pltpu.VMEM((4, 256, M), bf16),
                pltpu.VMEM((4, M, 256), bf16),
                pltpu.SemaphoreType.DMA((64,)),
            ],
        ),
        out_shape=[
            jax.ShapeDtypeStruct((2, rows, cols), f32),
            *[jax.ShapeDtypeStruct((2, M, M), f32)] * 5,
        ],
        compiler_params=pltpu.CompilerParams(vmem_limit_bytes=60 * 2**20),
        cost_estimate=pl.CostEstimate(flops=6 * 10**9, bytes_accessed=50 * 2**20, transcendentals=0),
        name="positions",
    )(off_rows, off_cols, *objects, probe, probe4, amps, *tables)


def order_kernel(a0, a1, a2, a3, out):
    def body(i, _):
        base = pl.multiple_of(i * 32, 32)
        lane = lax.broadcasted_iota(jnp.int32, (32, 128), 1)
        j, m = i // 4, i % 4
        parts = [a[0, pl.ds(128 * j + m, 32, stride=4), :] for a in (a0, a1, a2, a3)]
        for k in range(4):
            idx = (lane * 4 + k) % 128
            acc = jnp.take_along_axis(parts[0], idx, axis=1)
            for b in range(1, 4):
                acc = jnp.where(lane >= 32 * b, jnp.take_along_axis(parts[b], idx, axis=1), acc)
            out[0, pl.ds(base, 32), 128 * k:128 * (k + 1)] = acc
        return 0
    lax.fori_loop(0, M // 32, body, 0)


def ordered(amps):
    spec = pl.BlockSpec((1, M, M), lambda i: (i, 0, 0))
    part = lambda b: pl.BlockSpec((1, M, 128), lambda i: (i, 0, b))
    return pl.pallas_call(
        order_kernel, grid=(amps.shape[0],), in_specs=[part(b) for b in range(4)], out_specs=spec,
        out_shape=jax.ShapeDtypeStruct(amps.shape, jnp.float32), name="ordered",
        cost_estimate=pl.CostEstimate(flops=10**6, bytes_accessed=12 * 2**20, transcendentals=0),
    )(amps, amps, amps, amps)


def scan_pairs(step, middle=None):
    pairs = []
    for s in range(16):
        z, x = s // 4, s % 4
        z = (z - step) % 4 if x == middle else z
        pairs.append((s, 4 * z + (x + step) % 4))
    return pairs


def rows_below(value):
    return lax.ppermute(value, "scan", [(s, (s - 1) % 16) for s in range(16)])


def rows_above(value):
    return lax.ppermute(value, "scan", [(s, (s + 1) % 16) for s in range(16)])


def detour(value, step):
    stages = []
    for middle in (None, 1 if step > 0 else 2, None):
        value = lax.ppermute(value, "scan", scan_pairs(step, middle))
        stages.append(value)
    return stages


def after(value, *done):
    return lax.optimization_barrier((value, *done))[0]


def tile_shift(value, step):
    return lax.ppermute(value, "tile", [(t, (t + step) % 8) for t in range(8)])


def part(kind):
    s = lax.axis_index("scan")
    t = lax.axis_index("tile")
    return {"core": t % 2, "y": t // 2, "x": s % 4, "z": s // 4}[kind]


def part_pairs(kind, d):
    if kind == "core":
        return "tile", [(t, t ^ 1) for t in range(8)]
    if kind == "y":
        return "tile", [(t, (t // 2 + d) % 4 * 2 + t % 2) for t in range(8)]
    if kind == "x":
        return "scan", [(s, s // 4 * 4 + (s % 4 + d) % 4) for s in range(16)]
    return "scan", [(s, (s // 4 + d) % 4 * 4 + s % 4) for s in range(16)]


def scatter_sum(value, kind):
    n = 2 if kind == "core" else 4
    me = part(kind)
    size = value.shape[0] // n
    total = lax.dynamic_slice_in_dim(value, me * size, size, 0)
    for d in range(1, n):
        piece = lax.dynamic_slice_in_dim(value, (me + d) % n * size, size, 0)
        total = total + lax.ppermute(piece, *part_pairs(kind, d))
    return total


def exchange_sum(value, kind):
    total = value
    for d in range(1, 4):
        total = total + lax.ppermute(value, *part_pairs(kind, d))
    return total


def gather_parts(value, kind):
    n = 2 if kind == "core" else 4
    me = part(kind)
    size = value.shape[0]
    whole = jnp.zeros((n * size,) + value.shape[1:], value.dtype)
    whole = lax.dynamic_update_slice_in_dim(whole, value, me * size, 0)
    for d in range(1, n):
        piece = lax.ppermute(value, *part_pairs(kind, d))
        whole = lax.dynamic_update_slice_in_dim(whole, piece, (me - d) % n * size, 0)
    return whole


def body(object_planes, probe_planes, amplitudes, off_rows, off_cols):
    rows_here = object_planes.shape[1]
    cols_here = object_planes.shape[2]
    count = amplitudes.shape[0]
    near = rows_here * 3 // 4
    left = object_planes[:, :, :M]
    low_left = rows_below(left[:, :near])
    far_left = detour(left[:, near:], 1)[-1]
    low_right = rows_below(object_planes[:, :near, M:])
    far_right = detour(object_planes[:, near:, M:], 1)[-1]
    beside = tile_shift(left, -1)
    amps = ordered(amplitudes)
    low_left, amps = lax.optimization_barrier((low_left, amps))
    corner_near = tile_shift(low_left, -1)
    corner_far = tile_shift(far_left, -1)
    own, lower_left, lower_right, strip, corner, probe_sum = positions(
        off_rows, off_cols,
        (object_planes, low_left, far_left, low_right, far_right, beside, corner_near, corner_far),
        probe_planes, amps, kernel_tables())
    right_near = rows_above(lower_right[:, :near])
    right_hops = detour(lower_right[:, near:], -1)
    corner = tile_shift(corner, 1)
    summed = scatter_sum(probe_sum.reshape(2 * M, M), "core")
    summed = scatter_sum(after(summed, right_hops[0]), "y")
    strip = tile_shift(after(strip, summed), 1)
    summed = exchange_sum(after(summed, right_hops[1], corner), "z")
    summed = exchange_sum(after(summed, right_hops[2], right_near), "x")
    npos_total = count * lax.axis_size("scan") * lax.axis_size("tile")
    summed = summed / jnp.sqrt(jnp.float32(npos_total))
    lower_left = after(lower_left + corner, summed)
    left_near = rows_above(lower_left[:, :near])
    left_hops = detour(lower_left[:, near:], -1)
    summed = gather_parts(summed, "y")
    summed = gather_parts(after(summed, left_hops[0]), "core")
    right_far, left_far = right_hops[2], left_hops[2]
    arrived = jnp.concatenate([
        jnp.concatenate([left_near, left_far], axis=1) + strip,
        jnp.concatenate([right_near, right_far], axis=1),
    ], axis=2)
    return (own + arrived, summed.reshape(2, M, M))


def solution(mesh):
    in_specs = (
        P(None, "scan", "tile"),
        P(),
        P(("scan", "tile"), None, None),
        P(("scan", "tile")),
        P(("scan", "tile")),
    )
    out_specs = (P(None, "scan", "tile"), P())
    return jax.shard_map(body, mesh=mesh, in_specs=in_specs, out_specs=out_specs, check_vma=False)
```

```python
import jax
import jax.numpy as jnp
import ml_dtypes
import numpy as np
from jax import lax
from jax.sharding import PartitionSpec as P
from jax.experimental import pallas as pl
from jax.experimental.pallas import tpu as pltpu

M = 512
Q4 = 128


def kernel_tables():
    counter = np.arange(M, dtype=np.int64)
    product = counter[:, None] * counter[None, :] % M
    angles = product.astype(np.float32) * np.float32(2.0 * 3.141592653589793 / M)
    norm_scale = np.float32(1.0) / np.sqrt(np.float32(M))
    cosine, sine = np.cos(angles) * norm_scale, np.sin(angles) * norm_scale
    classes = range(4)
    first = np.concatenate([np.arange(m, Q4, 4) for m in classes])
    c, s = cosine[first], sine[first]
    left1 = np.stack([np.block([[c[:, m::4], s[:, m::4]], [-s[:, m::4], c[:, m::4]]]) for m in classes])
    right2 = []
    for m in classes:
        c, s = cosine[:, m::4], sine[:, m::4]
        right2.append(np.block([[c, -s], [s, c]]))
    right2 = np.stack(right2)
    c, s = cosine[:Q4], sine[:Q4]
    left3 = np.stack([np.block([[c[:, m::4], -s[:, m::4]], [s[:, m::4], c[:, m::4]]]) for m in classes])
    c, s = cosine[:, :Q4], sine[:, :Q4]
    right4 = np.stack([np.block([[c[m::4], s[m::4]], [-s[m::4], c[m::4]]]) for m in classes])
    return [jnp.asarray(t.astype(ml_dtypes.bfloat16)) for t in (left1, right2, left3, right4)]


def mm(a, b):
    return jnp.dot(a, b, preferred_element_type=jnp.float32)


def butterfly(e, sign):
    (r0, i0), (r1, i1), (r2, i2), (r3, i3) = e
    ar, ai, br, bi = r0 + r2, i0 + i2, r0 - r2, i0 - i2
    cr, ci, dr, di = r1 + r3, i1 + i3, r1 - r3, i1 - i3
    plus = (br - di, bi + dr)
    minus = (br + di, bi - dr)
    one, three = (plus, minus) if sign > 0 else (minus, plus)
    return [(ar + cr, ai + ci), one, (ar - cr, ai - ci), three]


def spans(pieces, vmem):
    for ref, row, col in pieces:
        for b in range(ref.shape[2] // 128):
            there = vmem.at[:, col // 128 + b, row:row + ref.shape[1], :]
            yield ref.at[:, :, 128 * b:128 * (b + 1)], there


def kernel(row_ref, col_ref, own, low_left, far_left, low_right, far_right, beside, corner_near, corner_far,
           probe, probe4, amp, left1, right2, left3, right4,
           g_own, g_left, g_right, g_right_end, g_beside, g_corner, psum,
           ext, grad, zs, ps, es, hs, qs, xs, gs, ws, sems):
    step = pl.program_id(0)
    last = pl.num_programs(0) - 1
    rows = own.shape[1]
    cols = own.shape[2]
    wide = ext.shape[1]
    near = rows + low_left.shape[1]
    inputs = (
        (own, 0, 0), (low_left, rows, 0), (far_left, near, 0), (low_right, rows, M), (far_right, near, M),
        (beside, 0, cols), (corner_near, rows, cols), (corner_far, near, cols),
    )
    half_rows = rows + M // 2
    outputs = (
        (g_right, rows, M), (g_right_end, half_rows, M), (g_corner, rows, cols), (g_left, rows, 0),
        (g_beside, 0, cols), (g_own, 0, 0),
    )

    now = lax.rem(step, 2)

    def corner_of(position):
        c = col_ref[position]
        return row_ref[position], c // 128, lax.rem(c, 128)

    def take(position, buffer, quarter):
        r, cb, dc = corner_of(position)
        size = 64
        keep = lax.broadcasted_iota(jnp.int32, (size, 128), 1) < 128 - dc
        for base in range(128 * quarter, 128 * (quarter + 1), size):
            for p in range(2):
                blocks = [
                    pltpu.roll(ext[p, cb + b, pl.ds(r + base, size), :], 128 - dc, 1) for b in range(5)
                ]
                for b in range(4):
                    zs[buffer, p, b, base:base + size, :] = jnp.where(keep, blocks[b], blocks[b + 1])

    @pl.when(step == 0)
    def _():
        for n, (src, dst) in enumerate(spans(inputs, ext)):
            pltpu.make_async_copy(src, dst, sems.at[n]).start()

        def clear(i, _):
            base = pl.multiple_of(i * 8, 8)
            for p in range(2):
                for b in range(wide):
                    grad[p, b, pl.ds(base, 8), :] = jnp.zeros((8, 128), jnp.float32)
            return 0
        lax.fori_loop(0, grad.shape[2] // 8, clear, 0)

        def clear2(i, _):
            base = pl.multiple_of(i * 8, 8)
            for p in range(2):
                psum[p, pl.ds(base, 8), :] = jnp.zeros((8, M), jnp.float32)
            return 0
        lax.fori_loop(0, M // 8, clear2, 0)
        def clear3(i, _):
            base = pl.multiple_of(i * 16, 16)
            for m in range(4):
                ws[m, pl.ds(base, 16), :] = jnp.zeros((16, 256), jnp.float32)
                for p in range(2):
                    zs[1, p, m, pl.ds(base, 16), :] = jnp.zeros((16, 128), jnp.float32)
            return 0
        lax.fori_loop(0, M // 16, clear3, 0)
        for n, (src, dst) in enumerate(spans(inputs, ext)):
            pltpu.make_async_copy(src, dst, sems.at[n]).wait()
        for quarter in range(4):
            take(0, 0, quarter)

    def psi(k):
        for base in range(0, Q4, 16):
            for m in range(4):
                for b in (2 * k, 2 * k + 1):
                    at = slice(128 * b, 128 * (b + 1))
                    zr = zs[now, 0, b, pl.ds(base * 4 + m, 16, stride=4), :]
                    zi = zs[now, 1, b, pl.ds(base * 4 + m, 16, stride=4), :]
                    pr = probe4[0, m, base:base + 16, at]
                    pi = probe4[1, m, base:base + 16, at]
                    ps[m, base:base + 16, at] = (pr * zr - pi * zi).astype(jnp.bfloat16)
                    ps[m, base + Q4:base + Q4 + 16, at] = (pr * zi + pi * zr).astype(jnp.bfloat16)

    def left(table, source, k):
        at = slice(256 * k, 256 * (k + 1))
        for m in range(4):
            es[k, m] = mm(table[m], source[m, :, at])

    def half(k):
        at = slice(256 * k, 256 * (k + 1))
        there = slice(M + 256 * k, M + 256 * (k + 1))
        for base in range(0, Q4, 16):
            e = [(es[k, m, base:base + 16, :], es[k, m, base + Q4:base + Q4 + 16, :]) for m in range(4)]
            for j, (re, im) in enumerate(butterfly(e, -1)):
                hs[base + Q4 * j:base + Q4 * j + 16, at] = re.astype(jnp.bfloat16)
                hs[base + Q4 * j:base + Q4 * j + 16, there] = im.astype(jnp.bfloat16)

    def far(n):
        qs[n] = mm(hs[...], right2[n])

    def chi(n):
        at = slice(Q4 * n, Q4 * (n + 1))
        for j in range(4):
            for m in range(4):
                rows_at = slice(128 * j + 32 * m, 128 * j + 32 * (m + 1))
                fr = qs[n, rows_at, 0:Q4]
                fi = qs[n, rows_at, Q4:]
                inverse = lax.rsqrt(fr * fr + fi * fi)
                factor = 1.0 - amp[0, rows_at, at] * jnp.minimum(inverse, 2.0)
                xs[m, 32 * j:32 * (j + 1), at] = (fr * factor).astype(jnp.bfloat16)
                xs[m, 32 * j + Q4:32 * (j + 1) + Q4, at] = (fi * factor).astype(jnp.bfloat16)

    def back(k):
        for base in range(0, Q4, 16):
            e = [(es[k, m, base:base + 16, :], es[k, m, base + Q4:base + Q4 + 16, :]) for m in range(4)]
            for j, (re, im) in enumerate(butterfly(e, 1)):
                re = re.astype(jnp.bfloat16)
                im = im.astype(jnp.bfloat16)
                for m in range(2):
                    there = slice(base + Q4 * j, base + Q4 * j + 16)
                    gs[2 * k + m, there, 0:Q4] = re[:, Q4 * m:Q4 * (m + 1)]
                    gs[2 * k + m, there, Q4:] = im[:, Q4 * m:Q4 * (m + 1)]

    def wave(n):
        ws[n] = mm(gs[n], right4[n])

    def finish(position, buffer, quarter):
        r, cb, dc = corner_of(position)
        size = 16
        keep = lax.broadcasted_iota(jnp.int32, (size, 128), 1) >= dc
        zero = jnp.zeros((size, 128), jnp.float32)
        for base in range(128 * quarter, 128 * (quarter + 1), size):
            at = slice(base, base + size)
            e = [(ws[m, at, 0:Q4], ws[m, at, Q4:]) for m in range(4)]
            old = [[grad[p, cb + b, pl.ds(r + base, size), :] for b in range(5)] for p in range(2)]
            rolled = ([zero], [zero])
            for j, (wr, wi) in enumerate(butterfly(e, 1)):
                there = slice(Q4 * j, Q4 * (j + 1))
                pr = probe[0, at, there]
                pi = probe[1, at, there]
                zr = zs[buffer, 0, j, at, :]
                zi = zs[buffer, 1, j, at, :]
                psum[0, at, there] += zr * wr + zi * wi
                psum[1, at, there] += zr * wi - zi * wr
                rolled[0].append(pltpu.roll(pr * wr + pi * wi, dc, 1))
                rolled[1].append(pltpu.roll(pr * wi - pi * wr, dc, 1))
            for p in range(2):
                u = rolled[p] + [zero]
                for b in range(5):
                    grad[p, cb + b, pl.ds(r + base, size), :] = old[p][b] + jnp.where(keep, u[b + 1], u[b])

    previous = jnp.maximum(step - 1, 0)

    @pl.when(step < last)
    def _():
        following = jnp.minimum(step + 1, last - 1)
        psi(0)
        left(left1, ps, 0)
        psi(1)
        half(0)
        left(left1, ps, 1)
        half(1)
        far(0)
        finish(previous, 1 - now, 0)
        far(1)
        finish(previous, 1 - now, 1)
        chi(0)
        far(2)
        finish(previous, 1 - now, 2)
        chi(1)
        far(3)
        finish(previous, 1 - now, 3)
        chi(2)
        left(left3, xs, 0)
        take(following, 1 - now, 0)
        chi(3)
        back(0)
        take(following, 1 - now, 1)
        left(left3, xs, 1)
        wave(0)
        wave(1)
        take(following, 1 - now, 2)
        back(1)
        wave(2)
        take(following, 1 - now, 3)
        wave(3)

    @pl.when(step == last)
    def _():
        for quarter in range(4):
            finish(previous, 1 - now, quarter)

    @pl.when(step == last)
    def _():
        for n, (dst, src) in enumerate(spans(outputs, grad)):
            pltpu.make_async_copy(src, dst, sems.at[n]).start()
        for n, (dst, src) in enumerate(spans(outputs, grad)):
            pltpu.make_async_copy(src, dst, sems.at[n]).wait()


def positions(off_rows, off_cols, objects, probe, amps, tables):
    count = amps.shape[0]
    rows, cols = objects[0].shape[1:]
    f32, bf16 = jnp.float32, jnp.bfloat16
    anyspec = pl.BlockSpec(memory_space=pl.ANY)
    whole = lambda shape: pl.BlockSpec(shape, lambda i, *_: (0,) * len(shape))
    probe4 = probe.reshape(2, Q4, 4, M).transpose(0, 2, 1, 3)
    return pl.pallas_call(
        kernel,
        grid_spec=pltpu.PrefetchScalarGridSpec(
            num_scalar_prefetch=2,
            grid=(count + 1,),
            in_specs=[
                *[anyspec] * len(objects),
                whole((2, M, M)), whole((2, 4, Q4, M)),
                pl.BlockSpec((1, M, M), lambda i, *_: (jnp.minimum(i, count - 1), 0, 0)),
                whole((4, 256, 256)), whole((4, 1024, 256)), whole((4, 256, 256)), whole((4, 256, 256)),
            ],
            out_specs=[*[anyspec] * 6, whole((2, M, M))],
            scratch_shapes=[
                pltpu.VMEM((2, (cols + M) // 128, rows + M, 128), f32),
                pltpu.VMEM((2, (cols + M) // 128, rows + M, 128), f32),
                pltpu.VMEM((2, 2, 4, M, 128), f32),
                pltpu.VMEM((4, 256, M), bf16),
                pltpu.VMEM((2, 4, 256, 256), f32),
                pltpu.VMEM((M, 2 * M), bf16),
                pltpu.VMEM((4, M, 256), f32),
                pltpu.VMEM((4, 256, M), bf16),
                pltpu.VMEM((4, M, 256), bf16),
                pltpu.VMEM((4, M, 256), f32),
                pltpu.SemaphoreType.DMA((64,)),
            ],
        ),
        out_shape=[
            jax.ShapeDtypeStruct((2, rows, cols), f32),
            *[jax.ShapeDtypeStruct((2, n, M), f32) for n in (M, M // 2, M // 2, M, M, M)],
        ],
        compiler_params=pltpu.CompilerParams(vmem_limit_bytes=60 * 2**20),
        cost_estimate=pl.CostEstimate(flops=6 * 10**9, bytes_accessed=50 * 2**20, transcendentals=0),
        name="positions",
    )(off_rows, off_cols, *objects, probe, probe4, amps, *tables)


def order_kernel(a0, a1, a2, a3, out):
    def body(i, _):
        base = pl.multiple_of(i * 32, 32)
        lane = lax.broadcasted_iota(jnp.int32, (32, 128), 1)
        j, m = i // 4, i % 4
        parts = [a[0, pl.ds(128 * j + m, 32, stride=4), :] for a in (a0, a1, a2, a3)]
        for k in range(4):
            idx = (lane * 4 + k) % 128
            acc = jnp.take_along_axis(parts[0], idx, axis=1)
            for b in range(1, 4):
                acc = jnp.where(lane >= 32 * b, jnp.take_along_axis(parts[b], idx, axis=1), acc)
            out[0, pl.ds(base, 32), 128 * k:128 * (k + 1)] = acc
        return 0
    lax.fori_loop(0, M // 32, body, 0)


def ordered(amps):
    spec = pl.BlockSpec((1, M, M), lambda i: (i, 0, 0))
    part = lambda b: pl.BlockSpec((1, M, 128), lambda i: (i, 0, b))
    return pl.pallas_call(
        order_kernel, grid=(amps.shape[0],), in_specs=[part(b) for b in range(4)], out_specs=spec,
        out_shape=jax.ShapeDtypeStruct(amps.shape, jnp.float32), name="ordered",
        cost_estimate=pl.CostEstimate(flops=10**6, bytes_accessed=12 * 2**20, transcendentals=0),
    )(amps, amps, amps, amps)


def scan_pairs(step, middle=None):
    pairs = []
    for s in range(16):
        z, x = s // 4, s % 4
        z = (z - step) % 4 if x == middle else z
        pairs.append((s, 4 * z + (x + step) % 4))
    return pairs


def rows_below(value):
    return lax.ppermute(value, "scan", [(s, (s - 1) % 16) for s in range(16)])


def rows_above(value):
    return lax.ppermute(value, "scan", [(s, (s + 1) % 16) for s in range(16)])


def detour(value, step):
    stages = []
    for middle in (None, 1 if step > 0 else 2, None):
        value = lax.ppermute(value, "scan", scan_pairs(step, middle))
        stages.append(value)
    return stages


def after(value, *done):
    return lax.optimization_barrier((value, *done))[0]


def tile_shift(value, step):
    return lax.ppermute(value, "tile", [(t, (t + step) % 8) for t in range(8)])


def part(kind):
    s = lax.axis_index("scan")
    t = lax.axis_index("tile")
    return {"core": t % 2, "y": t // 2, "x": s % 4, "z": s // 4}[kind]


def part_pairs(kind, d):
    if kind == "core":
        return "tile", [(t, t ^ 1) for t in range(8)]
    if kind == "y":
        return "tile", [(t, (t // 2 + d) % 4 * 2 + t % 2) for t in range(8)]
    if kind == "x":
        return "scan", [(s, s // 4 * 4 + (s % 4 + d) % 4) for s in range(16)]
    return "scan", [(s, (s // 4 + d) % 4 * 4 + s % 4) for s in range(16)]


def scatter_sum(value, kind, *done):
    n = 2 if kind == "core" else 4
    me = part(kind)
    size = value.shape[0] // n
    total = lax.dynamic_slice_in_dim(value, me * size, size, 0)
    pieces = [
        lax.ppermute(lax.dynamic_slice_in_dim(value, (me + d) % n * size, size, 0), *part_pairs(kind, d))
        for d in range(1, n)
    ]
    return sum(after(pieces, *done), total)


def exchange_sum(value, kind):
    total = value
    for d in range(1, 4):
        total = total + lax.ppermute(value, *part_pairs(kind, d))
    return total


def gather_parts(value, kind, *done):
    n = 2 if kind == "core" else 4
    me = part(kind)
    size = value.shape[0]
    whole = jnp.zeros((n * size,) + value.shape[1:], value.dtype)
    whole = lax.dynamic_update_slice_in_dim(whole, value, me * size, 0)
    pieces = after([lax.ppermute(value, *part_pairs(kind, d)) for d in range(1, n)], *done)
    for d, piece in enumerate(pieces, 1):
        whole = lax.dynamic_update_slice_in_dim(whole, piece, (me - d) % n * size, 0)
    return whole


def gather_back(value, kind, *done):
    me = part(kind)
    size = value.shape[0]
    whole = jnp.zeros((4 * size,) + value.shape[1:], value.dtype)
    whole = lax.dynamic_update_slice_in_dim(whole, value, me * size, 0)
    for d in range(1, 4):
        if d == 3:
            value = after(value, *done)
        value = lax.ppermute(value, *part_pairs(kind, 3))
        whole = lax.dynamic_update_slice_in_dim(whole, value, (me + d) % 4 * size, 0)
    return whole


def add_part(own, parts, half):
    size = 128
    edges = [0]
    while edges[-1] * size < own.shape[1]:
        edges.append(edges[-1] + parts[len(edges) - 1].shape[1] // size)
    pieces = len(edges) - 1

    def kernel(old, *rest):
        *arrived, out = rest
        step = pl.program_id(0)
        total = arrived[0][...]
        for n in range(1, pieces):
            total = jnp.where(step < edges[n], total, arrived[n][...])
        for extra in arrived[pieces:]:
            total = total + extra[...]
        out[...] = old[...] + total

    def spec(first, last, col):
        return pl.BlockSpec((2, size, M), lambda i: (0, jnp.clip(i, first, last - 1) - first, col))

    here = spec(0, edges[-1], half)
    specs = [here] + [spec(edges[n], edges[n + 1], 0) for n in range(pieces)]
    specs += [spec(0, edges[-1], 0)] * (len(parts) - pieces)
    return pl.pallas_call(
        kernel, grid=(edges[-1],), in_specs=specs, out_specs=here,
        out_shape=jax.ShapeDtypeStruct(own.shape, own.dtype), input_output_aliases={0: 0}, name="add_part",
        cost_estimate=pl.CostEstimate(flops=10**6, bytes_accessed=6 * 2**20, transcendentals=0),
    )(own, *parts)


def body(object_planes, probe_planes, amplitudes, off_rows, off_cols):
    rows_here = object_planes.shape[1]
    cols_here = object_planes.shape[2]
    count = amplitudes.shape[0]
    near = rows_here * 3 // 4
    left = object_planes[:, :, :M]
    low_left = rows_below(left[:, :near])
    far_left = detour(left[:, near:], 1)[-1]
    low_right = rows_below(object_planes[:, :near, M:])
    far_right = detour(object_planes[:, near:, M:], 1)[-1]
    beside = tile_shift(left, -1)
    amps = ordered(amplitudes)
    low_left, amps = lax.optimization_barrier((low_left, amps))
    corner_near = tile_shift(low_left, -1)
    corner_far = tile_shift(far_left, -1)
    own, lower_left, right, right_end, strip, corner, probe_sum = positions(
        off_rows, off_cols,
        (object_planes, low_left, far_left, low_right, far_right, beside, corner_near, corner_far),
        probe_planes, amps, kernel_tables())
    together = lax.optimization_barrier
    right = rows_above(right)
    right_end = rows_above(right_end)
    corner = tile_shift(corner, 1)
    summed = scatter_sum(probe_sum.reshape(2 * M, M), "core")
    summed = scatter_sum(summed, "y", right)
    strip = tile_shift(after(strip, summed), 1)
    far = M * 3 // 4
    cuts = ((0, far), (far, M))
    *left, summed = together((*[lower_left[:, i:j] + corner[:, i:j] for i, j in cuts], summed))
    summed = scatter_sum(summed, "z", right_end)
    summed = exchange_sum(summed, "x")
    npos_total = count * lax.axis_size("scan") * lax.axis_size("tile")
    summed = summed / jnp.sqrt(jnp.float32(npos_total))
    *left, summed = together((*left, summed))
    hops = detour(left[1], -1)
    left = [rows_above(left[0]), hops[2]]
    summed = gather_back(summed, "z", hops[0])
    own = add_part(own, (right, right_end), 1)
    summed = gather_parts(summed, "y", hops[1])
    own = add_part(own, (strip,), 0)
    own, summed = together((own, summed))
    summed = gather_parts(after(summed, *left), "core")
    own = add_part(own, left, 0)
    return (own, summed.reshape(2, M, M))


def solution(mesh):
    in_specs = (
        P(None, "scan", "tile"),
        P(),
        P(("scan", "tile"), None, None),
        P(("scan", "tile")),
        P(("scan", "tile")),
    )
    out_specs = (P(None, "scan", "tile"), P())
    return jax.shard_map(body, mesh=mesh, in_specs=in_specs, out_specs=out_specs, check_vma=False)
```

```python
import jax
import jax.numpy as jnp
import ml_dtypes
import numpy as np
from jax import lax
from jax.sharding import PartitionSpec as P
from jax.experimental import pallas as pl
from jax.experimental.pallas import tpu as pltpu

M = 512
Q4 = 128


def kernel_tables():
    counter = np.arange(M, dtype=np.int64)
    product = counter[:, None] * counter[None, :] % M
    angles = product.astype(np.float32) * np.float32(2.0 * 3.141592653589793 / M)
    norm_scale = np.float32(1.0) / np.sqrt(np.float32(M))
    cosine, sine = np.cos(angles) * norm_scale, np.sin(angles) * norm_scale
    classes = range(4)
    first = np.concatenate([np.arange(m, Q4, 4) for m in classes])
    c, s = cosine[first], sine[first]
    left1 = np.stack([np.block([[c[:, m::4], s[:, m::4]], [-s[:, m::4], c[:, m::4]]]) for m in classes])
    right2 = []
    for m in classes:
        c, s = cosine[:, m::4], sine[:, m::4]
        right2.append(np.block([[c, -s], [s, c]]))
    right2 = np.stack(right2)
    c, s = cosine[:Q4], sine[:Q4]
    left3 = np.stack([np.block([[c[:, m::4], -s[:, m::4]], [s[:, m::4], c[:, m::4]]]) for m in classes])
    c, s = cosine[:, :Q4], sine[:, :Q4]
    right4 = np.stack([np.block([[c[m::4], s[m::4]], [-s[m::4], c[m::4]]]) for m in classes])
    return [jnp.asarray(t.astype(ml_dtypes.bfloat16)) for t in (left1, right2, left3, right4)]


def mm(a, b):
    return jnp.dot(a, b, preferred_element_type=jnp.float32)


def butterfly(e, sign):
    (r0, i0), (r1, i1), (r2, i2), (r3, i3) = e
    ar, ai, br, bi = r0 + r2, i0 + i2, r0 - r2, i0 - i2
    cr, ci, dr, di = r1 + r3, i1 + i3, r1 - r3, i1 - i3
    plus = (br - di, bi + dr)
    minus = (br + di, bi - dr)
    one, three = (plus, minus) if sign > 0 else (minus, plus)
    return [(ar + cr, ai + ci), one, (ar - cr, ai - ci), three]


def spans(pieces, vmem):
    for ref, row, col in pieces:
        for b in range(ref.shape[2] // 128):
            there = vmem.at[:, col // 128 + b, row:row + ref.shape[1], :]
            yield ref.at[:, :, 128 * b:128 * (b + 1)], there


def kernel(row_ref, col_ref, own, low_left, far_left, low_right, far_right, beside, corner_near, corner_far,
           probe, probe4, amp, left1, right2, left3, right4,
           g_own, g_left, g_right, g_right_end, g_beside, g_corner, psum,
           ext, grad, zs, ps, es, hs, qs, xs, gs, ws, sems):
    step = pl.program_id(0)
    last = pl.num_programs(0) - 1
    rows = own.shape[1]
    cols = own.shape[2]
    wide = ext.shape[1]
    near = rows + low_left.shape[1]
    inputs = (
        (own, 0, 0), (low_left, rows, 0), (far_left, near, 0), (low_right, rows, M), (far_right, near, M),
        (beside, 0, cols), (corner_near, rows, cols), (corner_far, near, cols),
    )
    outputs = (
        (g_right, rows, M), (g_right_end, rows + g_right.shape[1], M), (g_corner, rows, cols), (g_left, rows, 0),
        (g_beside, 0, cols), (g_own, 0, 0),
    )

    now = lax.rem(step, 2)

    def corner_of(position):
        c = col_ref[position]
        return row_ref[position], c // 128, lax.rem(c, 128)

    def take(position, buffer, quarter):
        r, cb, dc = corner_of(position)
        size = 64
        keep = lax.broadcasted_iota(jnp.int32, (size, 128), 1) < 128 - dc
        for base in range(128 * quarter, 128 * (quarter + 1), size):
            for p in range(2):
                blocks = [
                    pltpu.roll(ext[p, cb + b, pl.ds(r + base, size), :], 128 - dc, 1) for b in range(5)
                ]
                for b in range(4):
                    zs[buffer, p, b, base:base + size, :] = jnp.where(keep, blocks[b], blocks[b + 1])

    @pl.when(step == 0)
    def _():
        for n, (src, dst) in enumerate(spans(inputs, ext)):
            pltpu.make_async_copy(src, dst, sems.at[n]).start()

        def clear(i, _):
            base = pl.multiple_of(i * 8, 8)
            for p in range(2):
                for b in range(wide):
                    grad[p, b, pl.ds(base, 8), :] = jnp.zeros((8, 128), jnp.float32)
            return 0
        lax.fori_loop(0, grad.shape[2] // 8, clear, 0)

        def clear2(i, _):
            base = pl.multiple_of(i * 8, 8)
            for p in range(2):
                psum[p, pl.ds(base, 8), :] = jnp.zeros((8, M), jnp.float32)
            return 0
        lax.fori_loop(0, M // 8, clear2, 0)
        def clear3(i, _):
            base = pl.multiple_of(i * 16, 16)
            for m in range(4):
                ws[m, pl.ds(base, 16), :] = jnp.zeros((16, 256), jnp.float32)
                for p in range(2):
                    zs[1, p, m, pl.ds(base, 16), :] = jnp.zeros((16, 128), jnp.float32)
            return 0
        lax.fori_loop(0, M // 16, clear3, 0)
        for n, (src, dst) in enumerate(spans(inputs, ext)):
            pltpu.make_async_copy(src, dst, sems.at[n]).wait()
        for quarter in range(4):
            take(0, 0, quarter)

    def psi(k):
        for base in range(0, Q4, 16):
            for m in range(4):
                for b in (2 * k, 2 * k + 1):
                    at = slice(128 * b, 128 * (b + 1))
                    zr = zs[now, 0, b, pl.ds(base * 4 + m, 16, stride=4), :]
                    zi = zs[now, 1, b, pl.ds(base * 4 + m, 16, stride=4), :]
                    pr = probe4[0, m, base:base + 16, at]
                    pi = probe4[1, m, base:base + 16, at]
                    ps[m, base:base + 16, at] = (pr * zr - pi * zi).astype(jnp.bfloat16)
                    ps[m, base + Q4:base + Q4 + 16, at] = (pr * zi + pi * zr).astype(jnp.bfloat16)

    def left(table, source, k):
        at = slice(256 * k, 256 * (k + 1))
        for m in range(4):
            es[k, m] = mm(table[m], source[m, :, at])

    def half(k):
        at = slice(256 * k, 256 * (k + 1))
        there = slice(M + 256 * k, M + 256 * (k + 1))
        for base in range(0, Q4, 16):
            e = [(es[k, m, base:base + 16, :], es[k, m, base + Q4:base + Q4 + 16, :]) for m in range(4)]
            for j, (re, im) in enumerate(butterfly(e, -1)):
                hs[base + Q4 * j:base + Q4 * j + 16, at] = re.astype(jnp.bfloat16)
                hs[base + Q4 * j:base + Q4 * j + 16, there] = im.astype(jnp.bfloat16)

    def far(n):
        qs[n] = mm(hs[...], right2[n])

    def chi(n):
        at = slice(Q4 * n, Q4 * (n + 1))
        for j in range(4):
            for m in range(4):
                rows_at = slice(128 * j + 32 * m, 128 * j + 32 * (m + 1))
                fr = qs[n, rows_at, 0:Q4]
                fi = qs[n, rows_at, Q4:]
                inverse = lax.rsqrt(fr * fr + fi * fi)
                factor = 1.0 - amp[0, rows_at, at] * jnp.minimum(inverse, 2.0)
                xs[m, 32 * j:32 * (j + 1), at] = (fr * factor).astype(jnp.bfloat16)
                xs[m, 32 * j + Q4:32 * (j + 1) + Q4, at] = (fi * factor).astype(jnp.bfloat16)

    def back(k):
        for base in range(0, Q4, 16):
            e = [(es[k, m, base:base + 16, :], es[k, m, base + Q4:base + Q4 + 16, :]) for m in range(4)]
            for j, (re, im) in enumerate(butterfly(e, 1)):
                re = re.astype(jnp.bfloat16)
                im = im.astype(jnp.bfloat16)
                for m in range(2):
                    there = slice(base + Q4 * j, base + Q4 * j + 16)
                    gs[2 * k + m, there, 0:Q4] = re[:, Q4 * m:Q4 * (m + 1)]
                    gs[2 * k + m, there, Q4:] = im[:, Q4 * m:Q4 * (m + 1)]

    def wave(n):
        ws[n] = mm(gs[n], right4[n])

    def finish(position, buffer, quarter):
        r, cb, dc = corner_of(position)
        size = 16
        keep = lax.broadcasted_iota(jnp.int32, (size, 128), 1) >= dc
        zero = jnp.zeros((size, 128), jnp.float32)
        for base in range(128 * quarter, 128 * (quarter + 1), size):
            at = slice(base, base + size)
            e = [(ws[m, at, 0:Q4], ws[m, at, Q4:]) for m in range(4)]
            old = [[grad[p, cb + b, pl.ds(r + base, size), :] for b in range(5)] for p in range(2)]
            rolled = ([zero], [zero])
            for j, (wr, wi) in enumerate(butterfly(e, 1)):
                there = slice(Q4 * j, Q4 * (j + 1))
                pr = probe[0, at, there]
                pi = probe[1, at, there]
                zr = zs[buffer, 0, j, at, :]
                zi = zs[buffer, 1, j, at, :]
                psum[0, at, there] += zr * wr + zi * wi
                psum[1, at, there] += zr * wi - zi * wr
                rolled[0].append(pltpu.roll(pr * wr + pi * wi, dc, 1))
                rolled[1].append(pltpu.roll(pr * wi - pi * wr, dc, 1))
            for p in range(2):
                u = rolled[p] + [zero]
                for b in range(5):
                    grad[p, cb + b, pl.ds(r + base, size), :] = old[p][b] + jnp.where(keep, u[b + 1], u[b])

    previous = jnp.maximum(step - 1, 0)

    @pl.when(step < last)
    def _():
        following = jnp.minimum(step + 1, last - 1)
        psi(0)
        left(left1, ps, 0)
        psi(1)
        half(0)
        left(left1, ps, 1)
        half(1)
        far(0)
        finish(previous, 1 - now, 0)
        far(1)
        finish(previous, 1 - now, 1)
        chi(0)
        far(2)
        finish(previous, 1 - now, 2)
        chi(1)
        far(3)
        finish(previous, 1 - now, 3)
        chi(2)
        left(left3, xs, 0)
        take(following, 1 - now, 0)
        chi(3)
        back(0)
        take(following, 1 - now, 1)
        left(left3, xs, 1)
        wave(0)
        wave(1)
        take(following, 1 - now, 2)
        back(1)
        wave(2)
        take(following, 1 - now, 3)
        wave(3)

    @pl.when(step == last)
    def _():
        for quarter in range(4):
            finish(previous, 1 - now, quarter)

    @pl.when(step == last)
    def _():
        for n, (dst, src) in enumerate(spans(outputs, grad)):
            pltpu.make_async_copy(src, dst, sems.at[n]).start()
        for n, (dst, src) in enumerate(spans(outputs, grad)):
            pltpu.make_async_copy(src, dst, sems.at[n]).wait()


def positions(off_rows, off_cols, objects, probe, amps, tables):
    count = amps.shape[0]
    rows, cols = objects[0].shape[1:]
    f32, bf16 = jnp.float32, jnp.bfloat16
    anyspec = pl.BlockSpec(memory_space=pl.ANY)
    whole = lambda shape: pl.BlockSpec(shape, lambda i, *_: (0,) * len(shape))
    probe4 = probe.reshape(2, Q4, 4, M).transpose(0, 2, 1, 3)
    return pl.pallas_call(
        kernel,
        grid_spec=pltpu.PrefetchScalarGridSpec(
            num_scalar_prefetch=2,
            grid=(count + 1,),
            in_specs=[
                *[anyspec] * len(objects),
                whole((2, M, M)), whole((2, 4, Q4, M)),
                pl.BlockSpec((1, M, M), lambda i, *_: (jnp.minimum(i, count - 1), 0, 0)),
                whole((4, 256, 256)), whole((4, 1024, 256)), whole((4, 256, 256)), whole((4, 256, 256)),
            ],
            out_specs=[*[anyspec] * 6, whole((2, M, M))],
            scratch_shapes=[
                pltpu.VMEM((2, (cols + M) // 128, rows + M, 128), f32),
                pltpu.VMEM((2, (cols + M) // 128, rows + M, 128), f32),
                pltpu.VMEM((2, 2, 4, M, 128), f32),
                pltpu.VMEM((4, 256, M), bf16),
                pltpu.VMEM((2, 4, 256, 256), f32),
                pltpu.VMEM((M, 2 * M), bf16),
                pltpu.VMEM((4, M, 256), f32),
                pltpu.VMEM((4, 256, M), bf16),
                pltpu.VMEM((4, M, 256), bf16),
                pltpu.VMEM((4, M, 256), f32),
                pltpu.SemaphoreType.DMA((64,)),
            ],
        ),
        out_shape=[
            jax.ShapeDtypeStruct((2, rows, cols), f32),
            *[jax.ShapeDtypeStruct((2, n, M), f32) for n in (M, M // 4, M * 3 // 4, M, M, M)],
        ],
        compiler_params=pltpu.CompilerParams(vmem_limit_bytes=60 * 2**20),
        cost_estimate=pl.CostEstimate(flops=6 * 10**9, bytes_accessed=50 * 2**20, transcendentals=0),
        name="positions",
    )(off_rows, off_cols, *objects, probe, probe4, amps, *tables)


def order_kernel(a0, a1, a2, a3, out):
    def body(i, _):
        base = pl.multiple_of(i * 32, 32)
        lane = lax.broadcasted_iota(jnp.int32, (32, 128), 1)
        j, m = i // 4, i % 4
        parts = [a[0, pl.ds(128 * j + m, 32, stride=4), :] for a in (a0, a1, a2, a3)]
        for k in range(4):
            idx = (lane * 4 + k) % 128
            acc = jnp.take_along_axis(parts[0], idx, axis=1)
            for b in range(1, 4):
                acc = jnp.where(lane >= 32 * b, jnp.take_along_axis(parts[b], idx, axis=1), acc)
            out[0, pl.ds(base, 32), 128 * k:128 * (k + 1)] = acc
        return 0
    lax.fori_loop(0, M // 32, body, 0)


def ordered(amps):
    spec = pl.BlockSpec((1, M, M), lambda i: (i, 0, 0))
    part = lambda b: pl.BlockSpec((1, M, 128), lambda i: (i, 0, b))
    return pl.pallas_call(
        order_kernel, grid=(amps.shape[0],), in_specs=[part(b) for b in range(4)], out_specs=spec,
        out_shape=jax.ShapeDtypeStruct(amps.shape, jnp.float32), name="ordered",
        cost_estimate=pl.CostEstimate(flops=10**6, bytes_accessed=12 * 2**20, transcendentals=0),
    )(amps, amps, amps, amps)


def scan_pairs(step, middle=None):
    pairs = []
    for s in range(16):
        z, x = s // 4, s % 4
        z = (z - step) % 4 if x == middle else z
        pairs.append((s, 4 * z + (x + step) % 4))
    return pairs


def rows_below(value):
    return lax.ppermute(value, "scan", [(s, (s - 1) % 16) for s in range(16)])


def rows_above(value):
    return lax.ppermute(value, "scan", [(s, (s + 1) % 16) for s in range(16)])


def detour(value, step):
    stages = []
    for middle in (None, 1 if step > 0 else 2, None):
        value = lax.ppermute(value, "scan", scan_pairs(step, middle))
        stages.append(value)
    return stages


def after(value, *done):
    return lax.optimization_barrier((value, *done))[0]


def tile_shift(value, step):
    return lax.ppermute(value, "tile", [(t, (t + step) % 8) for t in range(8)])


def part(kind):
    s = lax.axis_index("scan")
    t = lax.axis_index("tile")
    return {"core": t % 2, "y": t // 2, "x": s % 4, "z": s // 4}[kind]


def part_pairs(kind, d):
    if kind == "core":
        return "tile", [(t, t ^ 1) for t in range(8)]
    if kind == "y":
        return "tile", [(t, (t // 2 + d) % 4 * 2 + t % 2) for t in range(8)]
    if kind == "x":
        return "scan", [(s, s // 4 * 4 + (s % 4 + d) % 4) for s in range(16)]
    return "scan", [(s, (s // 4 + d) % 4 * 4 + s % 4) for s in range(16)]


def scatter_sum(value, kind, *done):
    n = 2 if kind == "core" else 4
    me = part(kind)
    size = value.shape[0] // n
    total = lax.dynamic_slice_in_dim(value, me * size, size, 0)
    pieces = [
        lax.ppermute(lax.dynamic_slice_in_dim(value, (me + d) % n * size, size, 0), *part_pairs(kind, d))
        for d in range(1, n)
    ]
    return sum(after(pieces, *done), total)


def exchange_sum(value, kind):
    total = value
    for d in range(1, 4):
        total = total + lax.ppermute(value, *part_pairs(kind, d))
    return total


def gather_parts(value, kind, *done):
    n = 2 if kind == "core" else 4
    me = part(kind)
    size = value.shape[0]
    whole = jnp.zeros((n * size,) + value.shape[1:], value.dtype)
    whole = lax.dynamic_update_slice_in_dim(whole, value, me * size, 0)
    pieces = after([lax.ppermute(value, *part_pairs(kind, d)) for d in range(1, n)], *done)
    for d, piece in enumerate(pieces, 1):
        whole = lax.dynamic_update_slice_in_dim(whole, piece, (me - d) % n * size, 0)
    return whole


def gather_back(value, kind, *done):
    me = part(kind)
    size = value.shape[0]
    whole = jnp.zeros((4 * size,) + value.shape[1:], value.dtype)
    whole = lax.dynamic_update_slice_in_dim(whole, value, me * size, 0)
    for d in range(1, 4):
        if d == 3:
            value = after(value, *done)
        value = lax.ppermute(value, *part_pairs(kind, 3))
        whole = lax.dynamic_update_slice_in_dim(whole, value, (me + d) % 4 * size, 0)
    return whole


def add_part(own, parts, half):
    size = 128
    edges = [0]
    while edges[-1] * size < own.shape[1]:
        edges.append(edges[-1] + parts[len(edges) - 1].shape[1] // size)
    pieces = len(edges) - 1

    def kernel(old, *rest):
        *arrived, out = rest
        step = pl.program_id(0)
        total = arrived[0][...]
        for n in range(1, pieces):
            total = jnp.where(step < edges[n], total, arrived[n][...])
        for extra in arrived[pieces:]:
            total = total + extra[...]
        out[...] = old[...] + total

    def spec(first, last, col):
        return pl.BlockSpec((2, size, M), lambda i: (0, jnp.clip(i, first, last - 1) - first, col))

    here = spec(0, edges[-1], half)
    specs = [here] + [spec(edges[n], edges[n + 1], 0) for n in range(pieces)]
    specs += [spec(0, edges[-1], 0)] * (len(parts) - pieces)
    return pl.pallas_call(
        kernel, grid=(edges[-1],), in_specs=specs, out_specs=here,
        out_shape=jax.ShapeDtypeStruct(own.shape, own.dtype), input_output_aliases={0: 0}, name="add_part",
        cost_estimate=pl.CostEstimate(flops=10**6, bytes_accessed=6 * 2**20, transcendentals=0),
    )(own, *parts)


def body(object_planes, probe_planes, amplitudes, off_rows, off_cols):
    rows_here = object_planes.shape[1]
    cols_here = object_planes.shape[2]
    count = amplitudes.shape[0]
    near = rows_here * 3 // 4
    left = object_planes[:, :, :M]
    low_left = rows_below(left[:, :near])
    far_left = detour(left[:, near:], 1)[-1]
    low_right = rows_below(object_planes[:, :near, M:])
    far_right = detour(object_planes[:, near:, M:], 1)[-1]
    beside = tile_shift(left, -1)
    amps = ordered(amplitudes)
    low_left, amps = lax.optimization_barrier((low_left, amps))
    corner_near = tile_shift(low_left, -1)
    corner_far = tile_shift(far_left, -1)
    own, lower_left, right, right_end, strip, corner, probe_sum = positions(
        off_rows, off_cols,
        (object_planes, low_left, far_left, low_right, far_right, beside, corner_near, corner_far),
        probe_planes, amps, kernel_tables())
    together = lax.optimization_barrier
    right = rows_above(right)
    right_end = rows_above(right_end)
    corner = tile_shift(corner, 1)
    summed = scatter_sum(probe_sum.reshape(2 * M, M), "core", right)
    summed = scatter_sum(summed, "y")
    strip = tile_shift(after(strip, summed), 1)
    far = M * 3 // 4
    cuts = ((0, far), (far, M))
    *left, summed = together((*[lower_left[:, i:j] + corner[:, i:j] for i, j in cuts], summed))
    summed = scatter_sum(summed, "z", right_end)
    summed = exchange_sum(summed, "x")
    npos_total = count * lax.axis_size("scan") * lax.axis_size("tile")
    summed = summed / jnp.sqrt(jnp.float32(npos_total))
    *left, summed = together((*left, summed))
    hops = detour(left[1], -1)
    left = [rows_above(left[0]), hops[2]]
    summed = gather_back(summed, "z", hops[0])
    own = add_part(own, (right, right_end), 1)
    summed = gather_parts(summed, "y", hops[1])
    own = add_part(own, (strip,), 0)
    own, summed = together((own, summed))
    summed = gather_parts(after(summed, *left), "core")
    own = add_part(own, left, 0)
    return (own, summed.reshape(2, M, M))


def solution(mesh):
    in_specs = (
        P(None, "scan", "tile"),
        P(),
        P(("scan", "tile"), None, None),
        P(("scan", "tile")),
        P(("scan", "tile")),
    )
    out_specs = (P(None, "scan", "tile"), P())
    return jax.shard_map(body, mesh=mesh, in_specs=in_specs, out_specs=out_specs, check_vma=False)
```

```python
import jax
import jax.numpy as jnp
import ml_dtypes
import numpy as np
from jax import lax
from jax.sharding import PartitionSpec as P
from jax.experimental import pallas as pl
from jax.experimental.pallas import tpu as pltpu

M = 512
Q4 = 128


def kernel_tables():
    counter = np.arange(M, dtype=np.int64)
    product = counter[:, None] * counter[None, :] % M
    angles = product.astype(np.float32) * np.float32(2.0 * 3.141592653589793 / M)
    norm_scale = np.float32(1.0) / np.sqrt(np.float32(M))
    cosine, sine = np.cos(angles) * norm_scale, np.sin(angles) * norm_scale
    classes = range(4)
    first = np.concatenate([np.arange(m, Q4, 4) for m in classes])
    c, s = cosine[first], sine[first]
    left1 = np.stack([np.block([[c[:, m::4], s[:, m::4]], [-s[:, m::4], c[:, m::4]]]) for m in classes])
    right2 = []
    for m in classes:
        c, s = cosine[:, m::4], sine[:, m::4]
        right2.append(np.block([[c, -s], [s, c]]))
    right2 = np.stack(right2)
    c, s = cosine[:Q4], sine[:Q4]
    left3 = np.stack([np.block([[c[:, m::4], -s[:, m::4]], [s[:, m::4], c[:, m::4]]]) for m in classes])
    c, s = cosine[:, :Q4], sine[:, :Q4]
    right4 = np.stack([np.block([[c[m::4], s[m::4]], [-s[m::4], c[m::4]]]) for m in classes])
    return [jnp.asarray(t.astype(ml_dtypes.bfloat16)) for t in (left1, right2, left3, right4)]


def mm(a, b):
    return jnp.dot(a, b, preferred_element_type=jnp.float32)


def butterfly(e, sign):
    (r0, i0), (r1, i1), (r2, i2), (r3, i3) = e
    ar, ai, br, bi = r0 + r2, i0 + i2, r0 - r2, i0 - i2
    cr, ci, dr, di = r1 + r3, i1 + i3, r1 - r3, i1 - i3
    plus = (br - di, bi + dr)
    minus = (br + di, bi - dr)
    one, three = (plus, minus) if sign > 0 else (minus, plus)
    return [(ar + cr, ai + ci), one, (ar - cr, ai - ci), three]


def spans(pieces, vmem):
    for ref, row, col in pieces:
        for b in range(ref.shape[2] // 128):
            there = vmem.at[:, col // 128 + b, row:row + ref.shape[1], :]
            yield ref.at[:, :, 128 * b:128 * (b + 1)], there


def kernel(row_ref, col_ref, own, low_left, far_left, low_right, far_right, beside, corner_near, corner_far,
           probe, probe4, amp, left1, right2, left3, right4,
           g_own, g_left, g_right, g_right_far, g_beside, g_corner, psum,
           ext, grad, zs, ps, es, hs, qs, xs, gs, ws, sems):
    step = pl.program_id(0)
    last = pl.num_programs(0) - 1
    rows = own.shape[1]
    cols = own.shape[2]
    wide = ext.shape[1]
    near = rows + low_left.shape[1]
    inputs = (
        (own, 0, 0), (low_left, rows, 0), (far_left, near, 0), (low_right, rows, M), (far_right, near, M),
        (beside, 0, cols), (corner_near, rows, cols), (corner_far, near, cols),
    )
    outputs = (
        (g_right, rows, M), (g_right_far, rows + g_right.shape[1], M), (g_corner, rows, cols), (g_left, rows, 0),
        (g_beside, 0, cols), (g_own, 0, 0),
    )

    now = lax.rem(step, 2)

    def corner_of(position):
        c = col_ref[position]
        return row_ref[position], c // 128, lax.rem(c, 128)

    def take(position, buffer, quarter):
        r, cb, dc = corner_of(position)
        size = 64
        keep = lax.broadcasted_iota(jnp.int32, (size, 128), 1) < 128 - dc
        for base in range(128 * quarter, 128 * (quarter + 1), size):
            for p in range(2):
                blocks = [
                    pltpu.roll(ext[p, cb + b, pl.ds(r + base, size), :], 128 - dc, 1) for b in range(5)
                ]
                for b in range(4):
                    zs[buffer, p, b, base:base + size, :] = jnp.where(keep, blocks[b], blocks[b + 1])

    @pl.when(step == 0)
    def _():
        for n, (src, dst) in enumerate(spans(inputs, ext)):
            pltpu.make_async_copy(src, dst, sems.at[n]).start()

        def clear(i, _):
            base = pl.multiple_of(i * 8, 8)
            for p in range(2):
                for b in range(wide):
                    grad[p, b, pl.ds(base, 8), :] = jnp.zeros((8, 128), jnp.float32)
            return 0
        lax.fori_loop(0, grad.shape[2] // 8, clear, 0)

        def clear2(i, _):
            base = pl.multiple_of(i * 8, 8)
            for p in range(2):
                psum[p, pl.ds(base, 8), :] = jnp.zeros((8, M), jnp.float32)
            return 0
        lax.fori_loop(0, M // 8, clear2, 0)
        def clear3(i, _):
            base = pl.multiple_of(i * 16, 16)
            for m in range(4):
                ws[m, pl.ds(base, 16), :] = jnp.zeros((16, 256), jnp.float32)
                for p in range(2):
                    zs[1, p, m, pl.ds(base, 16), :] = jnp.zeros((16, 128), jnp.float32)
            return 0
        lax.fori_loop(0, M // 16, clear3, 0)
        for n, (src, dst) in enumerate(spans(inputs, ext)):
            pltpu.make_async_copy(src, dst, sems.at[n]).wait()
        for quarter in range(4):
            take(0, 0, quarter)

    def psi(k):
        for base in range(0, Q4, 16):
            for m in range(4):
                for b in (2 * k, 2 * k + 1):
                    at = slice(128 * b, 128 * (b + 1))
                    zr = zs[now, 0, b, pl.ds(base * 4 + m, 16, stride=4), :]
                    zi = zs[now, 1, b, pl.ds(base * 4 + m, 16, stride=4), :]
                    pr = probe4[0, m, base:base + 16, at]
                    pi = probe4[1, m, base:base + 16, at]
                    ps[m, base:base + 16, at] = (pr * zr - pi * zi).astype(jnp.bfloat16)
                    ps[m, base + Q4:base + Q4 + 16, at] = (pr * zi + pi * zr).astype(jnp.bfloat16)

    def left(table, source, k):
        at = slice(256 * k, 256 * (k + 1))
        for m in range(4):
            es[k, m] = mm(table[m], source[m, :, at])

    def half(k):
        at = slice(256 * k, 256 * (k + 1))
        there = slice(M + 256 * k, M + 256 * (k + 1))
        for base in range(0, Q4, 16):
            e = [(es[k, m, base:base + 16, :], es[k, m, base + Q4:base + Q4 + 16, :]) for m in range(4)]
            for j, (re, im) in enumerate(butterfly(e, -1)):
                hs[base + Q4 * j:base + Q4 * j + 16, at] = re.astype(jnp.bfloat16)
                hs[base + Q4 * j:base + Q4 * j + 16, there] = im.astype(jnp.bfloat16)

    def far(n):
        qs[n] = mm(hs[...], right2[n])

    def chi(n):
        at = slice(Q4 * n, Q4 * (n + 1))
        for j in range(4):
            for m in range(4):
                rows_at = slice(128 * j + 32 * m, 128 * j + 32 * (m + 1))
                fr = qs[n, rows_at, 0:Q4]
                fi = qs[n, rows_at, Q4:]
                inverse = lax.rsqrt(fr * fr + fi * fi)
                factor = 1.0 - amp[0, rows_at, at] * jnp.minimum(inverse, 2.0)
                xs[m, 32 * j:32 * (j + 1), at] = (fr * factor).astype(jnp.bfloat16)
                xs[m, 32 * j + Q4:32 * (j + 1) + Q4, at] = (fi * factor).astype(jnp.bfloat16)

    def back(k):
        for base in range(0, Q4, 16):
            e = [(es[k, m, base:base + 16, :], es[k, m, base + Q4:base + Q4 + 16, :]) for m in range(4)]
            for j, (re, im) in enumerate(butterfly(e, 1)):
                re = re.astype(jnp.bfloat16)
                im = im.astype(jnp.bfloat16)
                for m in range(2):
                    there = slice(base + Q4 * j, base + Q4 * j + 16)
                    gs[2 * k + m, there, 0:Q4] = re[:, Q4 * m:Q4 * (m + 1)]
                    gs[2 * k + m, there, Q4:] = im[:, Q4 * m:Q4 * (m + 1)]

    def wave(n):
        ws[n] = mm(gs[n], right4[n])

    def finish(position, buffer, quarter):
        r, cb, dc = corner_of(position)
        size = 16
        keep = lax.broadcasted_iota(jnp.int32, (size, 128), 1) >= dc
        zero = jnp.zeros((size, 128), jnp.float32)
        for base in range(128 * quarter, 128 * (quarter + 1), size):
            at = slice(base, base + size)
            e = [(ws[m, at, 0:Q4], ws[m, at, Q4:]) for m in range(4)]
            old = [[grad[p, cb + b, pl.ds(r + base, size), :] for b in range(5)] for p in range(2)]
            rolled = ([zero], [zero])
            for j, (wr, wi) in enumerate(butterfly(e, 1)):
                there = slice(Q4 * j, Q4 * (j + 1))
                pr = probe[0, at, there]
                pi = probe[1, at, there]
                zr = zs[buffer, 0, j, at, :]
                zi = zs[buffer, 1, j, at, :]
                psum[0, at, there] += zr * wr + zi * wi
                psum[1, at, there] += zr * wi - zi * wr
                rolled[0].append(pltpu.roll(pr * wr + pi * wi, dc, 1))
                rolled[1].append(pltpu.roll(pr * wi - pi * wr, dc, 1))
            for p in range(2):
                u = rolled[p] + [zero]
                for b in range(5):
                    grad[p, cb + b, pl.ds(r + base, size), :] = old[p][b] + jnp.where(keep, u[b + 1], u[b])

    previous = jnp.maximum(step - 1, 0)

    @pl.when(step < last)
    def _():
        following = jnp.minimum(step + 1, last - 1)
        psi(0)
        left(left1, ps, 0)
        psi(1)
        half(0)
        left(left1, ps, 1)
        half(1)
        far(0)
        finish(previous, 1 - now, 0)
        far(1)
        finish(previous, 1 - now, 1)
        chi(0)
        far(2)
        finish(previous, 1 - now, 2)
        chi(1)
        far(3)
        finish(previous, 1 - now, 3)
        chi(2)
        left(left3, xs, 0)
        take(following, 1 - now, 0)
        chi(3)
        back(0)
        take(following, 1 - now, 1)
        left(left3, xs, 1)
        wave(0)
        wave(1)
        take(following, 1 - now, 2)
        back(1)
        wave(2)
        take(following, 1 - now, 3)
        wave(3)

    @pl.when(step == last)
    def _():
        for quarter in range(4):
            finish(previous, 1 - now, quarter)

    @pl.when(step == last)
    def _():
        for n, (dst, src) in enumerate(spans(outputs, grad)):
            pltpu.make_async_copy(src, dst, sems.at[n]).start()
        for n, (dst, src) in enumerate(spans(outputs, grad)):
            pltpu.make_async_copy(src, dst, sems.at[n]).wait()


def positions(off_rows, off_cols, objects, probe, amps, tables):
    count = amps.shape[0]
    rows, cols = objects[0].shape[1:]
    f32, bf16 = jnp.float32, jnp.bfloat16
    anyspec = pl.BlockSpec(memory_space=pl.ANY)
    whole = lambda shape: pl.BlockSpec(shape, lambda i, *_: (0,) * len(shape))
    probe4 = probe.reshape(2, Q4, 4, M).transpose(0, 2, 1, 3)
    return pl.pallas_call(
        kernel,
        grid_spec=pltpu.PrefetchScalarGridSpec(
            num_scalar_prefetch=2,
            grid=(count + 1,),
            in_specs=[
                *[anyspec] * len(objects),
                whole((2, M, M)), whole((2, 4, Q4, M)),
                pl.BlockSpec((1, M, M), lambda i, *_: (jnp.minimum(i, count - 1), 0, 0)),
                whole((4, 256, 256)), whole((4, 1024, 256)), whole((4, 256, 256)), whole((4, 256, 256)),
            ],
            out_specs=[*[anyspec] * 6, whole((2, M, M))],
            scratch_shapes=[
                pltpu.VMEM((2, (cols + M) // 128, rows + M, 128), f32),
                pltpu.VMEM((2, (cols + M) // 128, rows + M, 128), f32),
                pltpu.VMEM((2, 2, 4, M, 128), f32),
                pltpu.VMEM((4, 256, M), bf16),
                pltpu.VMEM((2, 4, 256, 256), f32),
                pltpu.VMEM((M, 2 * M), bf16),
                pltpu.VMEM((4, M, 256), f32),
                pltpu.VMEM((4, 256, M), bf16),
                pltpu.VMEM((4, M, 256), bf16),
                pltpu.VMEM((4, M, 256), f32),
                pltpu.SemaphoreType.DMA((64,)),
            ],
        ),
        out_shape=[
            jax.ShapeDtypeStruct((2, rows, cols), f32),
            *[jax.ShapeDtypeStruct((2, n, M), f32) for n in (M, M * 3 // 4, M // 4, M, M, M)],
        ],
        compiler_params=pltpu.CompilerParams(vmem_limit_bytes=60 * 2**20),
        cost_estimate=pl.CostEstimate(flops=6 * 10**9, bytes_accessed=50 * 2**20, transcendentals=0),
        name="positions",
    )(off_rows, off_cols, *objects, probe, probe4, amps, *tables)


def order_kernel(a0, a1, a2, a3, out):
    def body(i, _):
        base = pl.multiple_of(i * 32, 32)
        lane = lax.broadcasted_iota(jnp.int32, (32, 128), 1)
        j, m = i // 4, i % 4
        parts = [a[0, pl.ds(128 * j + m, 32, stride=4), :] for a in (a0, a1, a2, a3)]
        for k in range(4):
            idx = (lane * 4 + k) % 128
            acc = jnp.take_along_axis(parts[0], idx, axis=1)
            for b in range(1, 4):
                acc = jnp.where(lane >= 32 * b, jnp.take_along_axis(parts[b], idx, axis=1), acc)
            out[0, pl.ds(base, 32), 128 * k:128 * (k + 1)] = acc
        return 0
    lax.fori_loop(0, M // 32, body, 0)


def ordered(amps):
    spec = pl.BlockSpec((1, M, M), lambda i: (i, 0, 0))
    part = lambda b: pl.BlockSpec((1, M, 128), lambda i: (i, 0, b))
    return pl.pallas_call(
        order_kernel, grid=(amps.shape[0],), in_specs=[part(b) for b in range(4)], out_specs=spec,
        out_shape=jax.ShapeDtypeStruct(amps.shape, jnp.float32), name="ordered",
        cost_estimate=pl.CostEstimate(flops=10**6, bytes_accessed=12 * 2**20, transcendentals=0),
    )(amps, amps, amps, amps)


def scan_pairs(step, middle=None):
    pairs = []
    for s in range(16):
        z, x = s // 4, s % 4
        z = (z - step) % 4 if x == middle else z
        pairs.append((s, 4 * z + (x + step) % 4))
    return pairs


def rows_below(value):
    return lax.ppermute(value, "scan", [(s, (s - 1) % 16) for s in range(16)])


def rows_above(value):
    return lax.ppermute(value, "scan", [(s, (s + 1) % 16) for s in range(16)])


def detour(value, step):
    stages = []
    for middle in (None, 1 if step > 0 else 2, None):
        value = lax.ppermute(value, "scan", scan_pairs(step, middle))
        stages.append(value)
    return stages


def after(value, *done):
    return lax.optimization_barrier((value, *done))[0]


def tile_shift(value, step):
    return lax.ppermute(value, "tile", [(t, (t + step) % 8) for t in range(8)])


def part(kind):
    s = lax.axis_index("scan")
    t = lax.axis_index("tile")
    return {"core": t % 2, "y": t // 2, "x": s % 4, "z": s // 4}[kind]


def part_pairs(kind, d):
    if kind == "core":
        return "tile", [(t, t ^ 1) for t in range(8)]
    if kind == "y":
        return "tile", [(t, (t // 2 + d) % 4 * 2 + t % 2) for t in range(8)]
    if kind == "x":
        return "scan", [(s, s // 4 * 4 + (s % 4 + d) % 4) for s in range(16)]
    return "scan", [(s, (s // 4 + d) % 4 * 4 + s % 4) for s in range(16)]


def scatter_sum(value, kind, *done):
    n = 2 if kind == "core" else 4
    me = part(kind)
    size = value.shape[0] // n
    total = lax.dynamic_slice_in_dim(value, me * size, size, 0)
    pieces = [
        lax.ppermute(lax.dynamic_slice_in_dim(value, (me + d) % n * size, size, 0), *part_pairs(kind, d))
        for d in range(1, n)
    ]
    return sum(after(pieces, *done), total)


def exchange_sum(value, kind):
    total = value
    for d in range(1, 4):
        total = total + lax.ppermute(value, *part_pairs(kind, d))
    return total


def gather_parts(value, kind, *done):
    n = 2 if kind == "core" else 4
    me = part(kind)
    size = value.shape[0]
    whole = jnp.zeros((n * size,) + value.shape[1:], value.dtype)
    whole = lax.dynamic_update_slice_in_dim(whole, value, me * size, 0)
    pieces = after([lax.ppermute(value, *part_pairs(kind, d)) for d in range(1, n)], *done)
    for d, piece in enumerate(pieces, 1):
        whole = lax.dynamic_update_slice_in_dim(whole, piece, (me - d) % n * size, 0)
    return whole


def gather_back(value, kind, *done):
    me = part(kind)
    size = value.shape[0]
    whole = jnp.zeros((4 * size,) + value.shape[1:], value.dtype)
    whole = lax.dynamic_update_slice_in_dim(whole, value, me * size, 0)
    for d in range(1, 4):
        if d == 3:
            value = after(value, *done)
        value = lax.ppermute(value, *part_pairs(kind, 3))
        whole = lax.dynamic_update_slice_in_dim(whole, value, (me + d) % 4 * size, 0)
    return whole


def add_part(own, parts, half):
    size = 128
    edges = [0]
    while edges[-1] * size < own.shape[1]:
        edges.append(edges[-1] + parts[len(edges) - 1].shape[1] // size)
    pieces = len(edges) - 1

    def kernel(old, *rest):
        *arrived, out = rest
        step = pl.program_id(0)
        total = arrived[0][...]
        for n in range(1, pieces):
            total = jnp.where(step < edges[n], total, arrived[n][...])
        for extra in arrived[pieces:]:
            total = total + extra[...]
        out[...] = old[...] + total

    def spec(first, last, col):
        return pl.BlockSpec((2, size, M), lambda i: (0, jnp.clip(i, first, last - 1) - first, col))

    here = spec(0, edges[-1], half)
    specs = [here] + [spec(edges[n], edges[n + 1], 0) for n in range(pieces)]
    specs += [spec(0, edges[-1], 0)] * (len(parts) - pieces)
    return pl.pallas_call(
        kernel, grid=(edges[-1],), in_specs=specs, out_specs=here,
        out_shape=jax.ShapeDtypeStruct(own.shape, own.dtype), input_output_aliases={0: 0}, name="add_part",
        cost_estimate=pl.CostEstimate(flops=10**6, bytes_accessed=6 * 2**20, transcendentals=0),
    )(own, *parts)


def body(object_planes, probe_planes, amplitudes, off_rows, off_cols):
    rows_here = object_planes.shape[1]
    cols_here = object_planes.shape[2]
    count = amplitudes.shape[0]
    near = rows_here * 3 // 4
    left = object_planes[:, :, :M]
    low_left = rows_below(left[:, :near])
    far_left = detour(left[:, near:], 1)[-1]
    low_right = rows_below(object_planes[:, :near, M:])
    far_right = detour(object_planes[:, near:, M:], 1)[-1]
    beside = tile_shift(left, -1)
    amps = ordered(amplitudes)
    low_left, amps = lax.optimization_barrier((low_left, amps))
    corner_near = tile_shift(low_left, -1)
    corner_far = tile_shift(far_left, -1)
    own, lower_left, right, right_far, strip, corner, probe_sum = positions(
        off_rows, off_cols,
        (object_planes, low_left, far_left, low_right, far_right, beside, corner_near, corner_far),
        probe_planes, amps, kernel_tables())
    together = lax.optimization_barrier
    right = rows_above(right)
    right_hops = detour(right_far, -1)
    corner = tile_shift(corner, 1)
    summed = scatter_sum(probe_sum.reshape(2 * M, M), "core", right_hops[0])
    far = M * 3 // 4
    left = [lower_left[:, i:j] + corner[:, i:j] for i, j in ((0, far), (far, M))]
    summed = scatter_sum(summed, "y", right_hops[1], right, left)
    strip = tile_shift(after(strip, summed), 1)
    summed = scatter_sum(summed, "z", right_hops[2])
    summed = exchange_sum(summed, "x")
    npos_total = count * lax.axis_size("scan") * lax.axis_size("tile")
    summed = summed / jnp.sqrt(jnp.float32(npos_total))
    *left, summed = together((*left, summed))
    hops = detour(left[1], -1)
    left = [rows_above(left[0]), hops[2]]
    summed = gather_back(summed, "z", hops[0])
    own = add_part(own, (right, right_hops[2]), 1)
    summed = gather_parts(summed, "y", hops[1])
    own = add_part(own, (strip,), 0)
    own, summed = together((own, summed))
    summed = gather_parts(after(summed, *left), "core")
    own = add_part(own, left, 0)
    return (own, summed.reshape(2, M, M))


def solution(mesh):
    in_specs = (
        P(None, "scan", "tile"),
        P(),
        P(("scan", "tile"), None, None),
        P(("scan", "tile")),
        P(("scan", "tile")),
    )
    out_specs = (P(None, "scan", "tile"), P())
    return jax.shard_map(body, mesh=mesh, in_specs=in_specs, out_specs=out_specs, check_vma=False)
```
